128 devices in a mesh: ens: 8 (over x, core), dom: 16 (over y, z).
Axes of the slice: x: 4, y: 4, z: 4, core: 2. Of those that a mesh axis runs over, the one named last changes fastest.
Arguments:
- obs_members: float32 [64, 256, 1024], P('dom', 'ens'), may hold values from -2.4 to 2.4
- innovations: float32 [64, 1024], P('dom'), may hold values from -24 to 24
- error_inverse: float32 [64, 1024], P('dom'), may hold values from 0.5 to 2
- loc_table: float32 [64], replicated, may hold values from 0.2 to 1
- counts: int32 [16, 5], replicated, may hold values from 0 to 4, as said below
- block_picks: int32 [16, 5, 4], replicated, may hold values from 0 to 3, as said below
- loc_index: int32 [16, 32, 5, 4], P('dom', 'ens'), may hold values from 0 to 63
- background: float32 [16, 32, 256, 1024], P('dom', 'ens'), may hold values from -6 to 6
Outputs:
- analysis: float32 [16, 32, 256, 1024], P('dom', 'ens')
The draws below stay inside these ranges and needn't reach their ends.
Inputs may be any that keep to these rules, and one draw needn't show every extreme that they name: counts[t, 2] is 4 for every tile t, and in every draw one tile has 4 in every entry. Each block_picks[t, o, :] is a permutation of 0 .. 3.
All inputs are finite; a program needn't handle non-finite values.
Results may differ from the reference program's by a relative error of at most 0.0003.
Values sent between devices are 32-bit elements; how exact they have to be, the bound alone decides.
No kernel may reach another device: no remote copies, remote signals or barrier semaphores. Data moves between devices by JAX's collectives and lax.ppermute only.
A program may use at most 192 MiB of HBM per device.

```python
import math
import jax
import jax.numpy as jnp
from jax import lax

MEMBERS = 256
BLOCK_CAP = 4
OBS_BLOCK = 1024
REACH = 2
LOC_BINS = 64
NS_STEPS = 6
OFFSETS = 5
SLOTS = 20
TILES = 16
POINTS = 32
NBLOCKS = 64
CELLS = 1024


def draw_counts(key, part):
    key = jax.random.fold_in(key, 11)
    key_low, key_high, key_hot = jax.random.split(key, 3)
    draw_low = jax.random.randint(key_low, (TILES, OFFSETS), 0, BLOCK_CAP + 1)
    draw_high = jax.random.randint(key_high, (TILES, OFFSETS), 0, BLOCK_CAP + 1)
    granted = jnp.minimum(draw_low, draw_high)
    busiest = jax.random.randint(key_hot, (), 0, TILES)
    tile_rows = lax.broadcasted_iota(jnp.int32, (TILES, OFFSETS), 0)
    columns = lax.broadcasted_iota(jnp.int32, (TILES, OFFSETS), 1)
    saturated = (tile_rows == busiest) | (columns == REACH)
    return jnp.where(saturated, BLOCK_CAP, granted).astype(jnp.int32)


def draw_block_picks(key, part):
    key = jax.random.fold_in(key, 12)
    scores = jax.random.randint(key, (TILES, OFFSETS, BLOCK_CAP), 0, 1 << 20)
    ranks = lax.broadcasted_iota(jnp.int32, (TILES, OFFSETS, BLOCK_CAP), 2)
    distinct = scores * BLOCK_CAP + ranks
    return jnp.argsort(distinct, axis=-1, stable=True).astype(jnp.int32)


def plant(result, stream_key, low, high):
    shape = result.shape
    index_at = [jax.random.randint(jax.random.fold_in(stream_key, axis), (), 0, shape[axis]) for axis in range(len(shape))]
    result = result.at[tuple(index_at)].set(low)
    longest = shape.index(max(shape))
    index_at[longest] = (index_at[longest] + 1) % shape[longest]
    return result.at[tuple(index_at)].set(high)


def levels(stream_key, dims, cuts, smallest, high):
    level = 1.0
    for position, blocks in cuts:
        draws = jax.random.uniform(jax.random.fold_in(jax.random.fold_in(stream_key, 6), position), (blocks,), jnp.float32, smallest / len(cuts), high / len(cuts))
        level = level * jnp.repeat(jnp.exp(draws), dims[position] // blocks).reshape((-1,) + (1,) * (len(dims) - 1 - position))
    return level


def scatter_about(own_key, shape, scale, bound, pieces=(), kind=jnp.bfloat16):
    result = jax.random.normal(own_key, shape, jnp.float32) * scale
    if len(pieces) > 0:
        result = levels(own_key, shape, pieces, -0.22, 0.18) * result
    return jnp.clip(result, min=-bound, max=bound).astype(kind)


def setup_inputs(seed: int = 0) -> dict:
    splits = jax.random.split(jax.random.key(seed), 9)
    return {
        "obs_members": scatter_about(splits[0], (NBLOCKS, MEMBERS, OBS_BLOCK), 0.4, 2.4, ((0, 16), (1, 8)), jnp.float32),
        "innovations": scatter_about(splits[1], (NBLOCKS, OBS_BLOCK), 4.0, 24.0, ((0, 16),), jnp.float32),
        "error_inverse": jnp.clip(jnp.exp(math.log(2.0) - 1.3862944 * jax.random.uniform(splits[2], (NBLOCKS, OBS_BLOCK), jnp.float32) ** levels(splits[2], (NBLOCKS, OBS_BLOCK), ((0, 16),), -0.2, 0.2)), 0.5, 2.0),
        "loc_table": jnp.clip(jnp.exp(jax.random.uniform(splits[3], (LOC_BINS,), jnp.float32, math.log(0.2), math.log(1.0))), 0.2, 1.0),
        "counts": draw_counts(jax.random.fold_in(splits[8], 71), 0),
        "block_picks": draw_block_picks(jax.random.fold_in(splits[8], 71), 0),
        "loc_index": plant(jax.random.randint(splits[6], (TILES, POINTS, OFFSETS, BLOCK_CAP), 0, LOC_BINS), jax.random.fold_in(splits[6], 1), 0, LOC_BINS - 1).astype(jnp.int32),
        "background": scatter_about(splits[7], (TILES, POINTS, MEMBERS, CELLS), 1.0, 6.0, ((0, 16), (1, 8)), jnp.float32),
    }


precise = lax.Precision.HIGHEST

def root_transform(gram_sum, drive_sum):
    identity = jnp.eye(MEMBERS, dtype=jnp.float32)
    system = (MEMBERS - 1.0) * identity + gram_sum
    norm_scale = jnp.sqrt(jnp.sum(system * system))
    root_y = system / norm_scale
    root_q = identity
    for iteration in range(NS_STEPS):
        half_step = 1.5 * identity - 0.5 * jnp.matmul(root_q, root_y, precision=precise)
        root_y = jnp.matmul(root_y, half_step, precision=precise)
        root_q = jnp.matmul(half_step, root_q, precision=precise)
    spread = jnp.sqrt((MEMBERS - 1.0) / norm_scale) * root_q
    inner = jnp.matmul(root_q, drive_sum, precision=precise)
    mean_weights = jnp.matmul(root_q, inner, precision=precise) / norm_scale
    return spread + mean_weights[:, None]

def reference(obs_members, innovations, error_inverse, loc_table, counts, block_picks, loc_index, background):

    def one_tile(tile_index):
        member_parts = []
        innov_parts = []
        inverse_parts = []
        for offset in range(OFFSETS):
            owner_tile = (tile_index + offset - REACH) % TILES
            block_ids = (owner_tile * BLOCK_CAP + block_picks[tile_index, offset]).astype(jnp.int32)
            member_parts.append(jnp.take(obs_members, block_ids, axis=0))
            innov_parts.append(jnp.take(innovations, block_ids, axis=0))
            inverse_parts.append(jnp.take(error_inverse, block_ids, axis=0))
        members = jnp.concatenate(member_parts, axis=0)
        innov_slots = jnp.concatenate(innov_parts, axis=0)
        inverse = jnp.concatenate(inverse_parts, axis=0)
        live_mask = jnp.arange(BLOCK_CAP, dtype=jnp.int32)[None, :] < counts[tile_index][:, None]
        table_weight = loc_table[loc_index[tile_index]]
        slot_weight = jnp.where(live_mask[None], table_weight, 0.0).reshape(POINTS, SLOTS)

        def one_point(inputs):
            weight_row, background_rows = inputs
            obs_weight = weight_row[:, None] * inverse
            weighted = members * obs_weight[:, None, :]
            gram_sum = jnp.einsum('skn,sln->kl', weighted, members, precision=precise)
            drive_sum = jnp.einsum('skn,sn->k', weighted, innov_slots, precision=precise)
            transform = root_transform(gram_sum, drive_sum)
            return jnp.matmul(transform.T, background_rows, precision=precise)
        return lax.map(one_point, (slot_weight, background[tile_index]))
    return lax.map(one_tile, jnp.arange(TILES, dtype=jnp.int32))
```

```python
import jax
import jax.numpy as jnp
from jax import lax
from jax.experimental import pallas as pl
from jax.experimental.pallas import tpu as pltpu
from jax.sharding import PartitionSpec as P

F32 = jnp.float32
BF16 = jnp.bfloat16
HALF_ROWS = 136
NT = (((1,), (1,)), ((), ()))
NN = (((1,), (0,)), ((), ()))


def split2(value):
    high = value.astype(BF16)
    low = (value - high.astype(F32)).astype(BF16)
    return high, low


def dot3(left, right, dims=NN):
    def one(a, b):
        return lax.dot_general(a, b, dims, preferred_element_type=F32)

    return one(left[0], right[0]) + (one(left[0], right[1]) + one(left[1], right[0]))


def iota2(shape, axis):
    return lax.broadcasted_iota(jnp.int32, shape, axis)


def block_kernel(*refs):
    parts = refs[:8]
    inverse_ref, innov_ref, out_ref, high_ref, low_ref = refs[8:]
    place = lax.axis_index("ens")
    chip, core = place // 2, lax.rem(place, 2)
    for index, part in enumerate(parts):
        side = core if index < 4 else 1 - core
        row = pl.multiple_of(side * 128 + lax.rem(chip + 4 - index % 4, 4) * 32, 32)
        high, low = split2(part[...])
        high_ref[pl.ds(row, 32), :] = high
        low_ref[pl.ds(row, 32), :] = low
    inverse = inverse_ref[pl.ds(chip, 1), :]
    innov = innov_ref[pl.ds(chip, 1), :]

    def rows(start, count):
        at = pl.ds(start if isinstance(start, int) else pl.multiple_of(start, 64), count)
        return high_ref[at, :], low_ref[at, :]

    def weighted(pair):
        return split2((pair[0].astype(F32) + pair[1].astype(F32)) * inverse)

    own = rows(core * 128, 128)
    square = dot3(weighted(own), own, NT)
    cross = dot3(weighted(rows(core * 64, 64)), rows(128, 128), NT)
    pull = split2(jnp.broadcast_to(inverse * innov, (16, innov.shape[1])))
    drive = dot3(pull, own, NT)[0:1]
    top = square[:64]
    bottom = pltpu.roll(square[64:], 64, 1)
    row, col = iota2((64, 128), 0), iota2((64, 128), 1)
    packed = jnp.where((col < 64) & (col > row), bottom, top)
    diagonal = jnp.sum(jnp.where(row == col, bottom, 0.0), axis=0, keepdims=True)
    extra_row = iota2((8, 128), 0)
    extra = jnp.where(extra_row == 0, diagonal, jnp.where(extra_row == 1, drive, 0.0))
    out_ref[0:64, :] = packed
    out_ref[64:128, :] = cross
    out_ref[128:136, :] = extra


def combine_kernel(weight_ref, own_ref, first_ref, second_ref, third_ref, mine_ref, other_ref):
    sources = (own_ref, first_ref, second_ref, third_ref)

    def band(step, carry):
        at = pl.ds(pl.multiple_of(step * 8, 8), 8)
        tiles = [source[slot, at, :] for source in sources for slot in range(5)]
        for point in range(8):
            total = tiles[0] * weight_ref[point, 0]
            for slot in range(1, 20):
                total += tiles[slot] * weight_ref[point, slot]
            if point < 4:
                mine_ref[point, at, :] = total
            else:
                other_ref[point - 4, at, :] = total
        return carry

    lax.fori_loop(0, HALF_ROWS // 8, band, 0)


def unpack_square(packed, diagonal):
    row, col = iota2((64, 128), 0), iota2((64, 128), 1)
    flipped = jnp.transpose(jnp.concatenate([packed, jnp.zeros_like(packed)], axis=0))
    top = jnp.where((col < 64) & (col > row), flipped[:64], packed)
    upper = pltpu.roll(packed, 64, 1)
    lower = pltpu.roll(flipped[:64], 64, 1)
    middle = jnp.broadcast_to(pltpu.roll(diagonal, 64, 1)[0:1], (64, 128))
    shifted = col - 64
    corner = jnp.where(shifted > row, upper, jnp.where(shifted < row, lower, middle))
    bottom = jnp.where(col < 64, flipped[64:], corner)
    return jnp.concatenate([top, bottom], axis=0)


def analysis_kernel(mine_ref, theirs_ref, back_ref, out_ref, held, made, in_sem, out_sem):
    points = back_ref.shape[0]

    def chunks():
        for chip in range(4):
            for side in range(2):
                yield chip * 2 + side, (chip * 2 + side) * 32, side * 128 + chip * 32

    def fetch(point, index, outer, inner):
        return pltpu.make_async_copy(
            back_ref.at[point, pl.ds(outer, 32), :],
            held.at[point, pl.ds(inner, 32), :],
            in_sem.at[point, index],
        )

    def leave(point, index, outer, inner):
        return pltpu.make_async_copy(
            made.at[point, pl.ds(inner, 32), :],
            out_ref.at[point, pl.ds(outer, 32), :],
            out_sem.at[point, index],
        )

    for point in range(points):
        for chunk in chunks():
            fetch(point, *chunk).start()

    first = lax.rem(lax.axis_index("ens"), 2) == 0
    identity = (iota2((256, 256), 0) == iota2((256, 256), 1)).astype(F32)
    every = range(points)
    start, scale, drives = [], [], []
    for point in every:
        mine, theirs = mine_ref[point], theirs_ref[point]
        low = jnp.where(first, mine, theirs)
        high = jnp.where(first, theirs, mine)
        cross = jnp.concatenate([low[64:128], high[64:128]], axis=0)
        gram = jnp.concatenate(
            [
                jnp.concatenate([unpack_square(low[:64], low[128:136]), cross], axis=1),
                jnp.concatenate(
                    [jnp.transpose(cross), unpack_square(high[:64], high[128:136])], axis=1
                ),
            ],
            axis=0,
        )
        system = 255.0 * identity + gram
        inverse_norm = lax.rsqrt(jnp.sum(system * system, axis=(0, 1), keepdims=True))
        start.append(system * inverse_norm)
        scale.append(inverse_norm)
        drives.append(jnp.concatenate([low[129:130], high[129:130]], axis=1))

    def two_steps(value, pair):
        squared = [dot3(pair[i], pair[i]) for i in every]
        squared_pair = [split2(squared[i]) for i in every]
        rest = [
            split2(1.6875 * identity - 0.5625 * value[i] + 0.0625 * squared[i]) for i in every
        ]
        return [
            dot3(squared_pair[i], rest[i]) + (2.25 * identity - 2.4375 * value[i]) for i in every
        ]

    pair = [split2(start[i]) for i in every]
    root = two_steps(start, pair)
    root_pair = [split2(root[i]) for i in every]
    value = [dot3(split2(dot3(pair[i], root_pair[i])), root_pair[i]) for i in every]
    pair = [split2(value[i]) for i in every]
    factor_pair = [split2(f) for f in two_steps(value, pair)]
    root_pair = [split2(dot3(factor_pair[i], root_pair[i])) for i in every]
    value = [dot3(split2(dot3(pair[i], factor_pair[i])), factor_pair[i]) for i in every]
    pair = [split2(value[i]) for i in every]
    factor_pair = [split2(f) for f in two_steps(value, pair)]
    root = [dot3(factor_pair[i], root_pair[i]) for i in every]
    for point in every:
        inner = jnp.sum(root[point] * drives[point], axis=1, keepdims=True)
        mean = jnp.sum(root[point] * inner, axis=0, keepdims=True) * scale[point]
        transform = split2(jnp.sqrt(255.0 * scale[point]) * root[point] + mean)
        for chunk in chunks():
            fetch(point, *chunk).wait()
        for part in range(4):
            lanes = pl.ds(part * 256, 256)
            made[point, :, lanes] = dot3(transform, split2(held[point, :, lanes]))
        for chunk in chunks():
            leave(point, *chunk).start()
    for point in every:
        for chunk in chunks():
            leave(point, *chunk).wait()


def along_x(value, steps, swap=0):
    pairs = [(e, ((e // 2 + steps) % 4) * 2 + ((e % 2) ^ swap)) for e in range(8)]
    return lax.ppermute(value, "ens", pairs)


def along_dom(value, steps):
    return lax.ppermute(value, "dom", [(s, (s + steps) % 16) for s in range(16)])


def other_core(value):
    return along_x(value, 0, 1)


def point_weights(loc_table, counts, block_picks, loc_index, tile, chip):
    own_counts = lax.dynamic_index_in_dim(counts, tile, 0, keepdims=False)
    own_picks = lax.dynamic_index_in_dim(block_picks, tile, 0, keepdims=False)
    bins = jnp.arange(loc_table.shape[0], dtype=jnp.int32)
    table = jnp.sum(
        jnp.where(loc_index[..., None] == bins, loc_table, 0.0), axis=-1
    )
    live = jnp.arange(4, dtype=jnp.int32)[None, :] < own_counts[:, None]
    block = lax.rem(chip + 4 - jnp.arange(4, dtype=jnp.int32), 4)
    chosen = live[None] & (own_picks[None] == block[:, None, None])
    weight = jnp.sum(jnp.where(chosen[None], table[:, None], 0.0), axis=-1)
    return weight.reshape(loc_index.shape[0], 20)


def local(
    obs_members, innovations, error_inverse, loc_table, counts, block_picks, loc_index, background
):
    place = lax.axis_index("ens")
    tile = lax.axis_index("dom")
    chip = place // 2
    vmem = pl.BlockSpec(memory_space=pltpu.VMEM)

    def block_of(steps):
        return lax.dynamic_index_in_dim(
            obs_members, lax.rem(chip + steps, 4), 0, keepdims=False
        )

    parts = [block_of(0)] + [along_x(block_of(steps), steps) for steps in (1, 2, 3)]
    parts = parts + [other_core(part) for part in parts]
    weight = point_weights(loc_table, counts, block_picks, loc_index[0], tile, chip)
    weight = jnp.concatenate([weight, other_core(weight)], axis=0)
    half = pl.pallas_call(
        block_kernel,
        out_shape=jax.ShapeDtypeStruct((HALF_ROWS, 128), F32),
        in_specs=[vmem] * 10,
        out_specs=vmem,
        scratch_shapes=[pltpu.VMEM((256, 1024), BF16), pltpu.VMEM((256, 1024), BF16)],
        compiler_params=pltpu.CompilerParams(vmem_limit_bytes=16 << 20),
        name="block_matrices",
    )(*parts, error_inverse, innovations)
    halves = jnp.stack([half if o == 2 else along_dom(half, 2 - o) for o in range(5)])
    arrived = [along_x(halves, steps) for steps in (1, 2, 3)]
    shape = jax.ShapeDtypeStruct((4, HALF_ROWS, 128), F32)
    mine, other = pl.pallas_call(
        combine_kernel,
        out_shape=(shape, shape),
        in_specs=[pl.BlockSpec(memory_space=pltpu.SMEM)] + [vmem] * 4,
        out_specs=(vmem, vmem),
        compiler_params=pltpu.CompilerParams(vmem_limit_bytes=16 << 20),
        name="combine_points",
    )(weight, halves, *arrived)
    theirs = other_core(other)
    points, members, cells = background.shape[1:]
    analysis = pl.pallas_call(
        analysis_kernel,
        out_shape=jax.ShapeDtypeStruct((points, members, cells), F32),
        in_specs=[vmem, vmem, pl.BlockSpec(memory_space=pl.ANY)],
        out_specs=pl.BlockSpec(memory_space=pl.ANY),
        scratch_shapes=[
            pltpu.VMEM((points, members, cells), F32),
            pltpu.VMEM((points, members, cells), F32),
            pltpu.SemaphoreType.DMA((points, 8)),
            pltpu.SemaphoreType.DMA((points, 8)),
        ],
        compiler_params=pltpu.CompilerParams(vmem_limit_bytes=40 << 20),
        name="root_and_analysis",
    )(mine, theirs, background[0])
    return analysis[None]


def solution(mesh):
    placed = (
        P("dom", "ens", None),
        P("dom", None),
        P("dom", None),
        P(),
        P(),
        P(),
        P("dom", "ens", None, None),
        P("dom", "ens", None, None),
    )
    return jax.shard_map(
        local, mesh=mesh, in_specs=placed, out_specs=P("dom", "ens", None, None), check_vma=False
    )
```

```python
import jax
import jax.numpy as jnp
from jax import lax
from jax.experimental import pallas as pl
from jax.experimental.pallas import tpu as pltpu
from jax.sharding import PartitionSpec as P

F32 = jnp.float32
BF16 = jnp.bfloat16
HALF_ROWS = 136
PACKED_ROWS = 2 * HALF_ROWS
NT = (((1,), (1,)), ((), ()))
NN = (((1,), (0,)), ((), ()))


def split2(value):
    high = value.astype(BF16)
    low = (value - high.astype(F32)).astype(BF16)
    return high, low


def dot3(left, right, dims=NN):
    def one(a, b):
        return lax.dot_general(a, b, dims, preferred_element_type=F32)

    return one(left[0], right[0]) + (one(left[0], right[1]) + one(left[1], right[0]))


def iota2(shape, axis):
    return lax.broadcasted_iota(jnp.int32, shape, axis)


def block_kernel(*refs):
    parts = refs[:8]
    scaled_ref, out_ref, high_ref, low_ref = refs[8:]
    place = lax.axis_index("ens")
    chip, core = place // 2, lax.rem(place, 2)
    for index, part in enumerate(parts):
        side = core if index < 4 else 1 - core
        row = pl.multiple_of(side * 128 + lax.rem(chip + (0, 3, 1, 2)[index % 4], 4) * 32, 32)
        high, low = split2(part[...])
        high_ref[pl.ds(row, 32), :] = high
        low_ref[pl.ds(row, 32), :] = low
    inverse = scaled_ref[0:1, :]

    def rows(start, count):
        at = pl.ds(start if isinstance(start, int) else pl.multiple_of(start, 64), count)
        return high_ref[at, :], low_ref[at, :]

    def weighted(pair):
        return split2((pair[0].astype(F32) + pair[1].astype(F32)) * inverse)

    pull = split2(jnp.broadcast_to(scaled_ref[1:2, :], (16, scaled_ref.shape[1])))
    pairs = [rows(0, 128), rows(128, 128)]
    heavy = [weighted(pair) for pair in pairs]
    across = dot3(heavy[0], pairs[1], NT)
    row, col = iota2((64, 128), 0), iota2((64, 128), 1)
    extra_row = iota2((8, 128), 0)
    for side in range(2):
        square = dot3(heavy[side], pairs[side], NT)
        drive = dot3(pull, pairs[side], NT)[0:1]
        top = square[:64]
        bottom = pltpu.roll(square[64:], 64, 1)
        base = side * HALF_ROWS
        out_ref[base : base + 64, :] = jnp.where((col < 64) & (col > row), bottom, top)
        out_ref[base + 64 : base + 128, :] = across[side * 64 : side * 64 + 64]
        diagonal = jnp.sum(jnp.where(row == col, bottom, 0.0), axis=0, keepdims=True)
        out_ref[base + 128 : base + 136, :] = jnp.where(
            extra_row == 0, diagonal, jnp.where(extra_row == 1, drive, 0.0)
        )


def combine_kernel(weight_ref, same, beside, far, far_near, far_opposite, out_ref):
    place = lax.axis_index("ens")
    chip, core = place // 2, lax.rem(place, 2)
    ahead = lax.rem(chip + 2, 4)
    near = lax.rem(chip + 3 - 2 * core, 4)
    swapped = lax.rem(chip + 1 + 2 * core, 4)
    tiles = [
        *[(beside.at[i], 1 + 2 * core, b) for i, b in enumerate((chip, near, swapped, ahead))],
        (far, 4 * core, chip),
        (far_near.at[0], 4 * core, near),
        (far_near.at[1], 4 - 4 * core, near),
        (far_opposite, 4 * core, ahead),
        (same.at[1], 2, near),
        (same.at[3 * core], 2, lax.rem(chip + 2 * core, 4)),
    ]

    for band in range(5):
        at = pl.ds(band * 56, 56 if band < 4 else 48)
        for pair in range(2):
            totals = [None, None]
            for ref, offset, block in tiles:
                tile = ref[at, :]
                for side in range(2):
                    term = tile * weight_ref[2 * pair + side, offset * 4 + block]
                    totals[side] = term if totals[side] is None else totals[side] + term
            for side in range(2):
                out_ref[2 * pair + side, at, :] = totals[side]


def unpack_square(packed, diagonal):
    row, col = iota2((64, 128), 0), iota2((64, 128), 1)
    flipped = jnp.transpose(jnp.concatenate([packed, jnp.zeros_like(packed)], axis=0))
    top = jnp.where((col < 64) & (col > row), flipped[:64], packed)
    upper = pltpu.roll(packed, 64, 1)
    lower = pltpu.roll(flipped[:64], 64, 1)
    middle = jnp.broadcast_to(pltpu.roll(diagonal, 64, 1)[0:1], (64, 128))
    shifted = col - 64
    corner = jnp.where(shifted > row, upper, jnp.where(shifted < row, lower, middle))
    bottom = jnp.where(col < 64, flipped[64:], corner)
    return jnp.concatenate([top, bottom], axis=0)


def analysis_kernel(mine_ref, theirs_ref, back_ref, out_ref, held, made, in_sem, out_sem):
    points = back_ref.shape[0]

    def chunks():
        for chip in range(4):
            for side in range(2):
                yield chip * 2 + side, (chip * 2 + side) * 32, side * 128 + chip * 32

    def fetch(point, index, outer, inner):
        return pltpu.make_async_copy(
            back_ref.at[point, pl.ds(outer, 32), :],
            held.at[point, pl.ds(inner, 32), :],
            in_sem.at[point, index],
        )

    def leave(point, index, outer, inner):
        return pltpu.make_async_copy(
            made.at[point, pl.ds(inner, 32), :],
            out_ref.at[point, pl.ds(outer, 32), :],
            out_sem.at[point, index],
        )

    for point in range(points):
        for chunk in chunks():
            fetch(point, *chunk).start()

    identity = (iota2((256, 256), 0) == iota2((256, 256), 1)).astype(F32)
    every = range(points)
    start, scale, drives = [], [], []
    for point in every:
        whole = mine_ref[point] + theirs_ref[point]
        low, high = whole[:HALF_ROWS], whole[HALF_ROWS:]
        cross = jnp.concatenate([low[64:128], high[64:128]], axis=0)
        gram = jnp.concatenate(
            [
                jnp.concatenate([unpack_square(low[:64], low[128:136]), cross], axis=1),
                jnp.concatenate(
                    [jnp.transpose(cross), unpack_square(high[:64], high[128:136])], axis=1
                ),
            ],
            axis=0,
        )
        system = 255.0 * identity + gram
        inverse_norm = lax.rsqrt(jnp.sum(system * system, axis=(0, 1), keepdims=True))
        start.append(system * inverse_norm)
        scale.append(inverse_norm)
        drives.append(jnp.concatenate([low[129:130], high[129:130]], axis=1))

    def two_steps(value, pair):
        squared = [dot3(pair[i], pair[i]) for i in every]
        squared_pair = [split2(squared[i]) for i in every]
        rest = [
            split2(1.6875 * identity - 0.5625 * value[i] + 0.0625 * squared[i]) for i in every
        ]
        return [
            dot3(squared_pair[i], rest[i]) + (2.25 * identity - 2.4375 * value[i]) for i in every
        ]

    pair = [split2(start[i]) for i in every]
    root = two_steps(start, pair)
    root_pair = [split2(root[i]) for i in every]
    value = [dot3(split2(dot3(pair[i], root_pair[i])), root_pair[i]) for i in every]
    pair = [split2(value[i]) for i in every]
    factor_pair = [split2(f) for f in two_steps(value, pair)]
    root_pair = [split2(dot3(factor_pair[i], root_pair[i])) for i in every]
    value = [dot3(split2(dot3(pair[i], factor_pair[i])), factor_pair[i]) for i in every]
    pair = [split2(value[i]) for i in every]
    factor_pair = [split2(f) for f in two_steps(value, pair)]
    root = [dot3(factor_pair[i], root_pair[i]) for i in every]
    for point in every:
        inner = jnp.sum(root[point] * drives[point], axis=1, keepdims=True)
        mean = jnp.sum(root[point] * inner, axis=0, keepdims=True) * scale[point]
        transform = split2(jnp.sqrt(255.0 * scale[point]) * root[point] + mean)
        for chunk in chunks():
            fetch(point, *chunk).wait()
        for part in range(4):
            lanes = pl.ds(part * 256, 256)
            made[point, :, lanes] = dot3(transform, split2(held[point, :, lanes]))
        for chunk in chunks():
            leave(point, *chunk).start()
    for point in every:
        for chunk in chunks():
            leave(point, *chunk).wait()


def along_x(value, steps, swap=0):
    pairs = [(e, ((e // 2 + steps) % 4) * 2 + ((e % 2) ^ swap)) for e in range(8)]
    return lax.ppermute(value, "ens", pairs)


def other_core(value):
    return along_x(value, 0, 1)


def both_ways(value, axis, steps):
    pairs = []
    for e in range(8):
        for t in range(16):
            way = steps if e % 2 == 0 else -steps
            if axis == "dom":
                pairs.append((e * 16 + t, e * 16 + (t + way) % 16))
            else:
                pairs.append((e * 16 + t, (((e // 2 + way) % 4) * 2 + e % 2) * 16 + t))
    return lax.ppermute(value, ("ens", "dom"), pairs)


def block_weights(loc_table, counts, block_picks, loc_index, tile):
    own_counts = lax.dynamic_index_in_dim(counts, tile, 0, keepdims=False)
    own_picks = lax.dynamic_index_in_dim(block_picks, tile, 0, keepdims=False)
    bins = jnp.arange(loc_table.shape[0], dtype=jnp.int32)
    four = jnp.arange(4, dtype=jnp.int32)
    live = four[None, :] < own_counts[:, None]
    chosen = live[:, None, :] & (own_picks[:, None, :] == four[None, :, None])
    hit = (loc_index[:, :, None, :, None] == bins) & chosen[None, ..., None]
    weight = jnp.sum(jnp.where(hit, loc_table, 0.0), axis=(3, 4))
    return weight.reshape(loc_index.shape[0], 20)


def local(
    obs_members, innovations, error_inverse, loc_table, counts, block_picks, loc_index, background
):
    place = lax.axis_index("ens")
    tile = lax.axis_index("dom")
    chip = place // 2
    vmem = pl.BlockSpec(memory_space=pltpu.VMEM)

    def block_of(steps):
        return lax.dynamic_index_in_dim(
            obs_members, lax.rem(chip + steps, 4), 0, keepdims=False
        )

    inverse = lax.dynamic_slice_in_dim(error_inverse, chip, 1, 0)
    pull = inverse * lax.dynamic_slice_in_dim(innovations, chip, 1, 0)
    scaled = jnp.concatenate([inverse, pull], axis=0)
    order = (1, 3, 2)
    sent = dict(zip(order, [along_x(block_of(steps), steps) for steps in order]))
    parts = [block_of(0)] + [sent[steps] for steps in order]
    parts = parts + [other_core(part) for part in parts]
    whole = pl.pallas_call(
        block_kernel,
        out_shape=jax.ShapeDtypeStruct((PACKED_ROWS, 128), F32),
        in_specs=[vmem] * 9,
        out_specs=vmem,
        scratch_shapes=[pltpu.VMEM((256, 1024), BF16), pltpu.VMEM((256, 1024), BF16)],
        compiler_params=pltpu.CompilerParams(vmem_limit_bytes=16 << 20),
        name="block_matrices",
    )(*parts, scaled)
    whole, local_index, counts, block_picks = lax.optimization_barrier(
        (whole, loc_index[0], counts, block_picks)
    )
    far = both_ways(whole, "dom", 2)
    near = both_ways(whole, "ens", 1)
    opposite = along_x(whole, 2)
    weight = block_weights(loc_table, counts, block_picks, local_index, tile)
    near, opposite, far, weight = lax.optimization_barrier((near, opposite, far, weight))
    same = jnp.stack([whole, near, other_core(near), opposite])
    far_both = jnp.stack([far, other_core(far)])
    weights = (weight, other_core(weight))
    same, far, far_both, weights = lax.optimization_barrier((same, far, far_both, weights))
    far_opposite = along_x(far, 2)
    far_near = both_ways(far_both, "ens", 1)
    beside = both_ways(same, "dom", 1)
    combine = pl.pallas_call(
        combine_kernel,
        out_shape=jax.ShapeDtypeStruct((4, PACKED_ROWS, 128), F32),
        in_specs=[pl.BlockSpec(memory_space=pltpu.SMEM)] + [vmem] * 5,
        out_specs=vmem,
        compiler_params=pltpu.CompilerParams(vmem_limit_bytes=16 << 20),
        cost_estimate=pl.CostEstimate(flops=6000000, bytes_accessed=2000000, transcendentals=0),
        name="combine_points",
    )
    sources = (same, beside, far, far_near, far_opposite)
    theirs = other_core(combine(weights[1], *sources))
    mine = combine(weights[0], *sources)
    points, members, cells = background.shape[1:]
    analysis = pl.pallas_call(
        analysis_kernel,
        out_shape=jax.ShapeDtypeStruct((points, members, cells), F32),
        in_specs=[vmem, vmem, pl.BlockSpec(memory_space=pltpu.HBM)],
        out_specs=pl.BlockSpec(memory_space=pltpu.HBM),
        scratch_shapes=[
            pltpu.VMEM((points, members, cells), F32),
            pltpu.VMEM((points, members, cells), F32),
            pltpu.SemaphoreType.DMA((points, 8)),
            pltpu.SemaphoreType.DMA((points, 8)),
        ],
        compiler_params=pltpu.CompilerParams(vmem_limit_bytes=52 << 20),
        name="root_and_analysis",
    )(mine, theirs, background[0])
    return analysis[None]


def solution(mesh):
    placed = (
        P("dom", "ens", None),
        P("dom", None),
        P("dom", None),
        P(),
        P(),
        P(),
        P("dom", "ens", None, None),
        P("dom", "ens", None, None),
    )
    return jax.shard_map(
        local, mesh=mesh, in_specs=placed, out_specs=P("dom", "ens", None, None), check_vma=False
    )
```

```python
import jax
import jax.numpy as jnp
from jax import lax
from jax.experimental import pallas as pl
from jax.experimental.pallas import tpu as pltpu
from jax.sharding import PartitionSpec as P

F32 = jnp.float32
BF16 = jnp.bfloat16
EXTRA = 256
PACKED_ROWS = EXTRA + 8
NT = (((1,), (1,)), ((), ()))
NN = (((1,), (0,)), ((), ()))


def split2(value):
    high = value.astype(BF16)
    low = (value - high.astype(F32)).astype(BF16)
    return high, low


def dot3(left, right, dims=NN):
    def one(a, b):
        return lax.dot_general(a, b, dims, preferred_element_type=F32)

    return one(left[0], right[0]) + (one(left[0], right[1]) + one(left[1], right[0]))


def dot3_rows(left, right):
    rows = left[0].shape[0]
    both = jnp.dot(jnp.concatenate(left, axis=0), right[0], preferred_element_type=F32)
    return both[:rows] + (both[rows:] + jnp.dot(left[0], right[1], preferred_element_type=F32))


def iota2(shape, axis):
    return lax.broadcasted_iota(jnp.int32, shape, axis)


def block_kernel(*refs):
    parts = refs[:8]
    scaled_ref, out_ref, high_ref, low_ref, heavy_high_ref, heavy_low_ref = refs[8:]
    place = lax.axis_index("ens")
    chip, core = place // 2, lax.rem(place, 2)
    inverse = scaled_ref[0:1, :]
    for index, part in enumerate(parts):
        side = core if index < 4 else 1 - core
        behind = lax.rem(chip + (0, 3, 1, 2)[index % 4], 4)
        at = pl.ds(pl.multiple_of(side * 128 + behind * 32, 32), 32)
        value = part[...]
        high_ref[at, :], low_ref[at, :] = split2(value)
        heavy_high_ref[at, :], heavy_low_ref[at, :] = split2(value * inverse)
    pull = split2(jnp.broadcast_to(scaled_ref[1:2, :], (16, scaled_ref.shape[1])))
    heavy = (
        jnp.concatenate([heavy_high_ref[...], pull[0]], axis=0),
        jnp.concatenate([heavy_low_ref[...], pull[1]], axis=0),
    )
    product = dot3(heavy, (high_ref[...], low_ref[...]), NT)
    row, col = iota2((64, 128), 0), iota2((64, 128), 1)
    extra_row = iota2((8, 128), 0)
    extra = jnp.zeros((8, 128), F32)
    for side in range(2):
        lanes = slice(side * 128, side * 128 + 128)
        top = product[side * 128 : side * 128 + 64, lanes]
        bottom = pltpu.roll(product[side * 128 + 64 : side * 128 + 128, lanes], 64, 1)
        base = side * 128
        out_ref[base : base + 64, :] = jnp.where((col < 64) & (col > row), bottom, top)
        out_ref[base + 64 : base + 128, :] = product[side * 64 : side * 64 + 64, 128:]
        diagonal = jnp.sum(jnp.where(row == col, bottom, 0.0), axis=0, keepdims=True)
        extra = jnp.where(extra_row == 2 * side, diagonal, extra)
        extra = jnp.where(extra_row == 2 * side + 1, product[256:257, lanes], extra)
    out_ref[EXTRA:PACKED_ROWS, :] = extra


def combine_kernel(weight_ref, same, beside, far, far_near, far_opposite, out_ref):
    place = lax.axis_index("ens")
    chip, core = place // 2, lax.rem(place, 2)
    ahead = lax.rem(chip + 2, 4)
    near = lax.rem(chip + 3 - 2 * core, 4)
    swapped = lax.rem(chip + 1 + 2 * core, 4)
    tiles = [
        *[(beside.at[i], 1 + 2 * core, b) for i, b in enumerate((chip, near, swapped, ahead))],
        (far, 4 * core, chip),
        (far_near.at[0], 4 * core, near),
        (far_near.at[1], 4 - 4 * core, near),
        (far_opposite, 4 * core, ahead),
        (same.at[1], 2, near),
        (same.at[3 * core], 2, lax.rem(chip + 2 * core, 4)),
    ]

    for band in range(5):
        at = pl.ds(band * 56, 56 if band < 4 else 40)
        for pair in range(2):
            totals = [None, None]
            for ref, offset, block in tiles:
                tile = ref[at, :]
                for side in range(2):
                    row = (2 * pair + side) * 20 + offset * 4 + block
                    term = tile * weight_ref[pl.ds(row, 1), :]
                    totals[side] = term if totals[side] is None else totals[side] + term
            for side in range(2):
                out_ref[2 * pair + side, at, :] = totals[side]


def unpack_square(packed, diagonal):
    row, col = iota2((64, 128), 0), iota2((64, 128), 1)
    flipped = jnp.transpose(jnp.concatenate([packed, jnp.zeros_like(packed)], axis=0))
    top = jnp.where((col < 64) & (col > row), flipped[:64], packed)
    upper = pltpu.roll(packed, 64, 1)
    lower = pltpu.roll(flipped[:64], 64, 1)
    middle = pltpu.roll(jnp.broadcast_to(diagonal, (64, 128)), 64, 1)
    shifted = col - 64
    corner = jnp.where(shifted > row, upper, jnp.where(shifted < row, lower, middle))
    bottom = jnp.where(col < 64, flipped[64:], corner)
    return jnp.concatenate([top, bottom], axis=0)


def analysis_kernel(mine_ref, theirs_ref, back_ref, out_ref, held, made, in_sem, out_sem):
    points = back_ref.shape[0]

    def chunks():
        for chip in range(4):
            for side in range(2):
                yield chip * 2 + side, (chip * 2 + side) * 32, side * 128 + chip * 32

    def fetch(point, index, outer, inner):
        return pltpu.make_async_copy(
            back_ref.at[point, pl.ds(outer, 32), :],
            held.at[point, pl.ds(inner, 32), :],
            in_sem.at[point, index],
        )

    def leave(point, index, outer, inner):
        return pltpu.make_async_copy(
            made.at[point, pl.ds(inner, 32), :],
            out_ref.at[point, pl.ds(outer, 32), :],
            out_sem.at[point, index],
        )

    for point in range(points):
        for chunk in chunks():
            fetch(point, *chunk).start()

    identity = (iota2((256, 256), 0) == iota2((256, 256), 1)).astype(F32)
    every = range(points)
    start, scale, drives, squares = [], [], [], []
    for point in every:
        whole = mine_ref[point] + theirs_ref[point]
        extra = whole[EXTRA:]
        cross = jnp.concatenate([whole[64:128], whole[192:256]], axis=0)
        corners = [unpack_square(whole[:64], extra[0:1]), unpack_square(whole[128:192], extra[2:3])]
        gram = jnp.concatenate(
            [
                jnp.concatenate([corners[0], cross], axis=1),
                jnp.concatenate([jnp.transpose(cross), corners[1]], axis=1),
            ],
            axis=0,
        )
        system = 255.0 * identity + gram
        inverse_norm = lax.rsqrt(jnp.sum(system * system, axis=(0, 1), keepdims=True))
        system_pair = split2(system)
        squares.append(dot3(system_pair, system_pair) * (inverse_norm * inverse_norm))
        start.append(system * inverse_norm)
        scale.append(inverse_norm)
        drives.append(jnp.concatenate([extra[1:2], extra[3:4]], axis=1))

    def two_steps(value, squared):
        squared_pair = [split2(squared[i]) for i in every]
        rest = [
            split2(1.6875 * identity - 0.5625 * value[i] + 0.0625 * squared[i]) for i in every
        ]
        return [
            dot3(squared_pair[i], rest[i]) + (2.25 * identity - 2.4375 * value[i]) for i in every
        ]

    pair = [split2(start[i]) for i in every]
    root = two_steps(start, squares)
    root_pair = [split2(root[i]) for i in every]
    value = [dot3(split2(dot3(pair[i], root_pair[i])), root_pair[i]) for i in every]
    pair = [split2(value[i]) for i in every]
    factor_pair = [split2(f) for f in two_steps(value, [dot3(pair[i], pair[i]) for i in every])]
    root_pair = [split2(dot3(factor_pair[i], root_pair[i])) for i in every]
    value = [dot3(split2(dot3(pair[i], factor_pair[i])), factor_pair[i]) for i in every]
    pair = [split2(value[i]) for i in every]
    for point in every:
        for chunk in chunks():
            fetch(point, *chunk).wait()
    factor_pair = [split2(f) for f in two_steps(value, [dot3(pair[i], pair[i]) for i in every])]
    root = [dot3(factor_pair[i], root_pair[i]) for i in every]
    for point in every:
        inner = jnp.sum(root[point] * drives[point], axis=1, keepdims=True)
        mean = jnp.sum(root[point] * inner, axis=0, keepdims=True) * scale[point]
        transform = split2(jnp.sqrt(255.0 * scale[point]) * root[point] + mean)
        for part in range(2):
            lanes = pl.ds(part * 512, 512)
            made[point, :, lanes] = dot3_rows(transform, split2(held[point, :, lanes]))
        for chunk in chunks():
            leave(point, *chunk).start()
    for point in every:
        for chunk in chunks():
            leave(point, *chunk).wait()


def along_x(value, steps, swap=0):
    pairs = [(e, ((e // 2 + steps) % 4) * 2 + ((e % 2) ^ swap)) for e in range(8)]
    return lax.ppermute(value, "ens", pairs)


def other_core(value):
    return along_x(value, 0, 1)


def both_ways(value, axis, steps):
    pairs = []
    for e in range(8):
        for t in range(16):
            way = steps if e % 2 == 0 else -steps
            if axis == "dom":
                pairs.append((e * 16 + t, e * 16 + (t + way) % 16))
            else:
                pairs.append((e * 16 + t, (((e // 2 + way) % 4) * 2 + e % 2) * 16 + t))
    return lax.ppermute(value, ("ens", "dom"), pairs)


def block_weights(loc_table, counts, own_picks, loc_index, tile):
    own_counts = lax.dynamic_index_in_dim(counts, tile, 0, keepdims=False)
    bins = jnp.arange(loc_table.shape[0], dtype=jnp.int32)
    four = jnp.arange(4, dtype=jnp.int32)
    live = four[None, :] < own_counts[:, None]
    chosen = live[:, None, :] & (own_picks[:, None, :] == four[None, :, None])
    hit = (loc_index[:, :, None, :, None] == bins) & chosen[None, ..., None]
    weight = jnp.sum(jnp.where(hit, loc_table, 0.0), axis=(3, 4))
    return weight.reshape(loc_index.shape[0], 20)


def local(
    obs_members, innovations, error_inverse, loc_table, counts, block_picks, loc_index, background
):
    place = lax.axis_index("ens")
    tile = lax.axis_index("dom")
    chip = place // 2
    vmem = pl.BlockSpec(memory_space=pltpu.VMEM)

    def block_of(blocks, steps):
        return lax.dynamic_index_in_dim(blocks, lax.rem(chip + steps, 4), 0, keepdims=False)

    inverse = lax.dynamic_slice_in_dim(error_inverse, chip, 1, 0)
    pull = inverse * lax.dynamic_slice_in_dim(innovations, chip, 1, 0)
    scaled = jnp.concatenate([inverse, pull], axis=0)
    order = (1, 3, 2)
    sent = [block_of(obs_members, steps) for steps in order]
    *sent, obs_members = lax.optimization_barrier((*sent, obs_members))
    parts = [block_of(obs_members, 0)] + [along_x(part, steps) for part, steps in zip(sent, order)]
    parts = parts + [other_core(part) for part in parts]
    whole = pl.pallas_call(
        block_kernel,
        out_shape=jax.ShapeDtypeStruct((PACKED_ROWS, 128), F32),
        in_specs=[vmem] * 9,
        out_specs=vmem,
        scratch_shapes=[pltpu.VMEM((256, 1024), BF16)] * 4,
        compiler_params=pltpu.CompilerParams(vmem_limit_bytes=16 << 20),
        name="block_matrices",
    )(*parts, scaled)
    whole, local_index, counts, block_picks = lax.optimization_barrier(
        (whole, loc_index[0], counts, block_picks)
    )
    far = both_ways(whole, "dom", 2)
    near = both_ways(whole, "ens", 1)
    own_picks = lax.dynamic_index_in_dim(block_picks, tile, 0, keepdims=False)
    later, own_picks = lax.optimization_barrier((whole, own_picks))
    opposite = along_x(later, 2)
    weight = block_weights(loc_table, counts, own_picks, local_index, tile)
    near, far = lax.optimization_barrier((near, far))
    near_swapped, far_swapped = other_core(near), other_core(far)
    weights = [
        jnp.broadcast_to(part.reshape(-1, 1), (part.size, 128))
        for part in (weight, other_core(weight))
    ]
    same = jnp.stack([whole, near, near_swapped, opposite])
    far_both = jnp.stack([far, far_swapped])
    same, far, far_both, weights = lax.optimization_barrier((same, far, far_both, weights))
    far_opposite = along_x(far, 2)
    far_near = both_ways(far_both, "ens", 1)
    beside = both_ways(same, "dom", 1)
    combine = pl.pallas_call(
        combine_kernel,
        out_shape=jax.ShapeDtypeStruct((4, PACKED_ROWS, 128), F32),
        in_specs=[vmem] * 6,
        out_specs=vmem,
        compiler_params=pltpu.CompilerParams(vmem_limit_bytes=16 << 20),
        cost_estimate=pl.CostEstimate(flops=6000000, bytes_accessed=2000000, transcendentals=0),
        name="combine_points",
    )
    sources = (same, beside, far, far_near, far_opposite)
    theirs = other_core(combine(weights[1], *sources))
    mine = combine(weights[0], *sources)
    points, members, cells = background.shape[1:]
    analysis = pl.pallas_call(
        analysis_kernel,
        out_shape=jax.ShapeDtypeStruct((points, members, cells), F32),
        in_specs=[vmem, vmem, pl.BlockSpec(memory_space=pltpu.HBM)],
        out_specs=pl.BlockSpec(memory_space=pltpu.HBM),
        scratch_shapes=[
            pltpu.VMEM((points, members, cells), F32),
            pltpu.VMEM((points, members, cells), F32),
            pltpu.SemaphoreType.DMA((points, 8)),
            pltpu.SemaphoreType.DMA((points, 8)),
        ],
        compiler_params=pltpu.CompilerParams(vmem_limit_bytes=52 << 20),
        name="root_and_analysis",
    )(mine, theirs, background[0])
    return analysis[None]


def solution(mesh):
    placed = (
        P("dom", "ens", None),
        P("dom", None),
        P("dom", None),
        P(),
        P(),
        P(),
        P("dom", "ens", None, None),
        P("dom", "ens", None, None),
    )
    return jax.shard_map(
        local, mesh=mesh, in_specs=placed, out_specs=P("dom", "ens", None, None), check_vma=False
    )
```

```python
import jax
import jax.numpy as jnp
from jax import lax
from jax.experimental import pallas as pl
from jax.experimental.pallas import tpu as pltpu
from jax.sharding import PartitionSpec as P

F32 = jnp.float32
BF16 = jnp.bfloat16
EXTRA = 256
PACKED_ROWS = EXTRA + 8
NT = (((1,), (1,)), ((), ()))
NN = (((1,), (0,)), ((), ()))


def split2(value):
    high = value.astype(BF16)
    low = (value - high.astype(F32)).astype(BF16)
    return high, low


def dot3(left, right, dims=NN):
    def one(a, b):
        return lax.dot_general(a, b, dims, preferred_element_type=F32)

    return one(left[0], right[0]) + (one(left[0], right[1]) + one(left[1], right[0]))


def dot3_rows(left, right):
    rows = left[0].shape[0]
    both = jnp.dot(jnp.concatenate(left, axis=0), right[0], preferred_element_type=F32)
    return both[:rows] + (both[rows:] + jnp.dot(left[0], right[1], preferred_element_type=F32))


def iota2(shape, axis):
    return lax.broadcasted_iota(jnp.int32, shape, axis)


def block_kernel(*refs):
    parts = refs[:8]
    scaled_ref, out_ref, high_ref, low_ref, heavy_high_ref, heavy_low_ref = refs[8:]
    place = lax.axis_index("ens")
    chip, core = place // 2, lax.rem(place, 2)
    inverse = scaled_ref[0:1, :]
    for index, part in enumerate(parts):
        side = core if index < 4 else 1 - core
        behind = lax.rem(chip + (0, 3, 1, 2)[index % 4], 4)
        at = pl.ds(pl.multiple_of(side * 128 + behind * 32, 32), 32)
        value = part[...]
        high_ref[at, :], low_ref[at, :] = split2(value)
        heavy_high_ref[at, :], heavy_low_ref[at, :] = split2(value * inverse)
    pull = split2(jnp.broadcast_to(scaled_ref[1:2, :], (16, scaled_ref.shape[1])))
    heavy = (
        jnp.concatenate([heavy_high_ref[...], pull[0]], axis=0),
        jnp.concatenate([heavy_low_ref[...], pull[1]], axis=0),
    )
    product = dot3(heavy, (high_ref[...], low_ref[...]), NT)
    row, col = iota2((64, 128), 0), iota2((64, 128), 1)
    extra_row = iota2((8, 128), 0)
    extra = jnp.zeros((8, 128), F32)
    for side in range(2):
        lanes = slice(side * 128, side * 128 + 128)
        top = product[side * 128 : side * 128 + 64, lanes]
        bottom = pltpu.roll(product[side * 128 + 64 : side * 128 + 128, lanes], 64, 1)
        base = side * 128
        out_ref[base : base + 64, :] = jnp.where((col < 64) & (col > row), bottom, top)
        out_ref[base + 64 : base + 128, :] = product[side * 64 : side * 64 + 64, 128:]
        diagonal = jnp.sum(jnp.where(row == col, bottom, 0.0), axis=0, keepdims=True)
        extra = jnp.where(extra_row == 2 * side, diagonal, extra)
        extra = jnp.where(extra_row == 2 * side + 1, product[256:257, lanes], extra)
    out_ref[EXTRA:PACKED_ROWS, :] = extra


def add_tiles(weight_ref, tiles, start_ref, out_ref):
    for band in range(5):
        at = pl.ds(band * 56, 56 if band < 4 else 40)
        for pair in range(2):
            totals = [None if start_ref is None else start_ref[2 * pair + side, at, :] for side in range(2)]
            for ref, offset, block in tiles:
                tile = ref[at, :]
                for side in range(2):
                    row = (2 * pair + side) * 20 + offset * 4 + block
                    term = tile * weight_ref[pl.ds(row, 1), :]
                    totals[side] = term if totals[side] is None else totals[side] + term
            for side in range(2):
                out_ref[2 * pair + side, at, :] = totals[side]


def places():
    place = lax.axis_index("ens")
    chip, core = place // 2, lax.rem(place, 2)
    near = lax.rem(chip + 3 - 2 * core, 4)
    swapped = lax.rem(chip + 1 + 2 * core, 4)
    return core, chip, near, swapped, lax.rem(chip + 2, 4)


def early_kernel(weight_ref, same, far, far_opposite, out_ref):
    core, chip, near, _, ahead = places()
    tiles = [
        (same.at[1], 2, near),
        (same.at[3 * core], 2, lax.rem(chip + 2 * core, 4)),
        (far, 4 * core, chip),
        (far_opposite, 4 * core, ahead),
    ]
    add_tiles(weight_ref, tiles, None, out_ref)


def late_kernel(weight_ref, start_ref, beside, far_near, out_ref):
    core, chip, near, swapped, ahead = places()
    tiles = [
        *[(beside.at[i], 1 + 2 * core, b) for i, b in enumerate((chip, near, swapped, ahead))],
        (far_near.at[0], 4 * core, near),
        (far_near.at[1], 4 - 4 * core, near),
    ]
    add_tiles(weight_ref, tiles, start_ref, out_ref)


def unpack_square(packed, diagonal):
    row, col = iota2((64, 128), 0), iota2((64, 128), 1)
    flipped = jnp.transpose(jnp.concatenate([packed, jnp.zeros_like(packed)], axis=0))
    top = jnp.where((col < 64) & (col > row), flipped[:64], packed)
    upper = pltpu.roll(packed, 64, 1)
    lower = pltpu.roll(flipped[:64], 64, 1)
    middle = pltpu.roll(jnp.broadcast_to(diagonal, (64, 128)), 64, 1)
    shifted = col - 64
    corner = jnp.where(shifted > row, upper, jnp.where(shifted < row, lower, middle))
    bottom = jnp.where(col < 64, flipped[64:], corner)
    return jnp.concatenate([top, bottom], axis=0)


def analysis_kernel(mine_ref, theirs_ref, back_ref, out_ref, held, made, in_sem, out_sem):
    points = back_ref.shape[0]

    def chunks():
        for chip in range(4):
            for side in range(2):
                yield chip * 2 + side, (chip * 2 + side) * 32, side * 128 + chip * 32

    def fetch(point, index, outer, inner):
        return pltpu.make_async_copy(
            back_ref.at[point, pl.ds(outer, 32), :],
            held.at[point, pl.ds(inner, 32), :],
            in_sem.at[point, index],
        )

    def leave(point, index, outer, inner):
        return pltpu.make_async_copy(
            made.at[point, pl.ds(inner, 32), :],
            out_ref.at[point, pl.ds(outer, 32), :],
            out_sem.at[point, index],
        )

    for point in range(points):
        for chunk in chunks():
            fetch(point, *chunk).start()

    identity = (iota2((256, 256), 0) == iota2((256, 256), 1)).astype(F32)
    every = range(points)
    start, scale, drives, squares = [], [], [], []
    for point in every:
        whole = mine_ref[point] + theirs_ref[point]
        extra = whole[EXTRA:]
        cross = jnp.concatenate([whole[64:128], whole[192:256]], axis=0)
        corners = [unpack_square(whole[:64], extra[0:1]), unpack_square(whole[128:192], extra[2:3])]
        gram = jnp.concatenate(
            [
                jnp.concatenate([corners[0], cross], axis=1),
                jnp.concatenate([jnp.transpose(cross), corners[1]], axis=1),
            ],
            axis=0,
        )
        system = 255.0 * identity + gram
        inverse_norm = lax.rsqrt(jnp.sum(system * system, axis=(0, 1), keepdims=True))
        system_pair = split2(system)
        squares.append(dot3(system_pair, system_pair) * (inverse_norm * inverse_norm))
        start.append(system * inverse_norm)
        scale.append(inverse_norm)
        drives.append(jnp.concatenate([extra[1:2], extra[3:4]], axis=1))

    def two_steps(value, squared):
        squared_pair = [split2(squared[i]) for i in every]
        rest = [
            split2(1.6875 * identity - 0.5625 * value[i] + 0.0625 * squared[i]) for i in every
        ]
        return [
            dot3(squared_pair[i], rest[i]) + (2.25 * identity - 2.4375 * value[i]) for i in every
        ]

    pair = [split2(start[i]) for i in every]
    root = two_steps(start, squares)
    root_pair = [split2(root[i]) for i in every]
    value = [dot3(split2(dot3(pair[i], root_pair[i])), root_pair[i]) for i in every]
    pair = [split2(value[i]) for i in every]
    factor_pair = [split2(f) for f in two_steps(value, [dot3(pair[i], pair[i]) for i in every])]
    root_pair = [split2(dot3(factor_pair[i], root_pair[i])) for i in every]
    value = [dot3(split2(dot3(pair[i], factor_pair[i])), factor_pair[i]) for i in every]
    pair = [split2(value[i]) for i in every]
    for point in every:
        for chunk in chunks():
            fetch(point, *chunk).wait()
    factor_pair = [split2(f) for f in two_steps(value, [dot3(pair[i], pair[i]) for i in every])]
    root = [dot3(factor_pair[i], root_pair[i]) for i in every]
    for point in every:
        inner = jnp.sum(root[point] * drives[point], axis=1, keepdims=True)
        mean = jnp.sum(root[point] * inner, axis=0, keepdims=True) * scale[point]
        transform = split2(jnp.sqrt(255.0 * scale[point]) * root[point] + mean)
        for part in range(2):
            lanes = pl.ds(part * 512, 512)
            made[point, :, lanes] = dot3_rows(transform, split2(held[point, :, lanes]))
        for chunk in chunks():
            leave(point, *chunk).start()
    for point in every:
        for chunk in chunks():
            leave(point, *chunk).wait()


def along_x(value, steps, swap=0):
    pairs = [(e, ((e // 2 + steps) % 4) * 2 + ((e % 2) ^ swap)) for e in range(8)]
    return lax.ppermute(value, "ens", pairs)


def other_core(value):
    return along_x(value, 0, 1)


def both_ways(value, axis, steps):
    pairs = []
    for e in range(8):
        for t in range(16):
            way = steps if e % 2 == 0 else -steps
            if axis == "dom":
                pairs.append((e * 16 + t, e * 16 + (t + way) % 16))
            else:
                pairs.append((e * 16 + t, (((e // 2 + way) % 4) * 2 + e % 2) * 16 + t))
    return lax.ppermute(value, ("ens", "dom"), pairs)


def block_weights(loc_table, counts, own_picks, loc_index, tile):
    own_counts = lax.dynamic_index_in_dim(counts, tile, 0, keepdims=False)
    bins = jnp.arange(loc_table.shape[0], dtype=jnp.int32)
    four = jnp.arange(4, dtype=jnp.int32)
    live = four[None, :] < own_counts[:, None]
    chosen = live[:, None, :] & (own_picks[:, None, :] == four[None, :, None])
    hit = (loc_index[:, :, None, :, None] == bins) & chosen[None, ..., None]
    weight = jnp.sum(jnp.where(hit, loc_table, 0.0), axis=(3, 4))
    return weight.reshape(loc_index.shape[0], 20)


def local(
    obs_members, innovations, error_inverse, loc_table, counts, block_picks, loc_index, background
):
    place = lax.axis_index("ens")
    tile = lax.axis_index("dom")
    chip = place // 2
    vmem = pl.BlockSpec(memory_space=pltpu.VMEM)

    def block_of(blocks, steps):
        return lax.dynamic_index_in_dim(blocks, lax.rem(chip + steps, 4), 0, keepdims=False)

    inverse = lax.dynamic_slice_in_dim(error_inverse, chip, 1, 0)
    pull = inverse * lax.dynamic_slice_in_dim(innovations, chip, 1, 0)
    scaled = jnp.concatenate([inverse, pull], axis=0)
    order = (1, 3, 2)
    own, *sent = [block_of(obs_members, steps) for steps in (0, *order)]
    own, *sent, loc_index, counts, block_picks = lax.optimization_barrier(
        (own, *sent, loc_index, counts, block_picks)
    )
    parts = [own] + [along_x(part, steps) for part, steps in zip(sent, order)]
    parts = parts + [other_core(part) for part in parts]
    own_picks = lax.dynamic_index_in_dim(block_picks, tile, 0, keepdims=False)
    weight = block_weights(loc_table, counts, own_picks, loc_index[0], tile)
    scaled, weight = lax.optimization_barrier((scaled, weight))
    whole = pl.pallas_call(
        block_kernel,
        out_shape=jax.ShapeDtypeStruct((PACKED_ROWS, 128), F32),
        in_specs=[vmem] * 9,
        out_specs=vmem,
        scratch_shapes=[pltpu.VMEM((256, 1024), BF16)] * 4,
        compiler_params=pltpu.CompilerParams(vmem_limit_bytes=16 << 20),
        name="block_matrices",
    )(*parts, scaled)
    far = both_ways(whole, "dom", 2)
    near = both_ways(whole, "ens", 1)
    opposite = along_x(whole, 2)
    weight = jnp.broadcast_to(weight.reshape(-1, 1), (weight.size, 128))
    weights = [weight, other_core(weight)]
    near, far, opposite, weights = lax.optimization_barrier((near, far, opposite, weights))
    near_swapped, far_swapped = other_core(near), other_core(far)
    same = jnp.stack([whole, near, near_swapped, opposite])
    far_both = jnp.stack([far, far_swapped])
    same, far, far_both = lax.optimization_barrier((same, far, far_both))
    far_opposite = along_x(far, 2)
    far_near = both_ways(far_both, "ens", 1)
    beside = both_ways(same, "dom", 1)
    def combine(kernel, flops, *operands):
        return pl.pallas_call(
            kernel,
            out_shape=jax.ShapeDtypeStruct((4, PACKED_ROWS, 128), F32),
            in_specs=[vmem] * len(operands),
            out_specs=vmem,
            compiler_params=pltpu.CompilerParams(vmem_limit_bytes=16 << 20),
            cost_estimate=pl.CostEstimate(flops=flops, bytes_accessed=2000000, transcendentals=0),
            name=kernel.__name__,
        )(*operands)

    started = [combine(early_kernel, 2000000, part, same, far, far_opposite) for part in weights]
    theirs = other_core(combine(late_kernel, 2000000, weights[1], started[1], beside, far_near))
    mine = combine(late_kernel, 2000000, weights[0], started[0], beside, far_near)
    points, members, cells = background.shape[1:]
    analysis = pl.pallas_call(
        analysis_kernel,
        out_shape=jax.ShapeDtypeStruct((points, members, cells), F32),
        in_specs=[vmem, vmem, pl.BlockSpec(memory_space=pltpu.HBM)],
        out_specs=pl.BlockSpec(memory_space=pltpu.HBM),
        scratch_shapes=[
            pltpu.VMEM((points, members, cells), F32),
            pltpu.VMEM((points, members, cells), F32),
            pltpu.SemaphoreType.DMA((points, 8)),
            pltpu.SemaphoreType.DMA((points, 8)),
        ],
        compiler_params=pltpu.CompilerParams(vmem_limit_bytes=52 << 20),
        name="root_and_analysis",
    )(mine, theirs, background[0])
    return analysis[None]


def solution(mesh):
    placed = (
        P("dom", "ens", None),
        P("dom", None),
        P("dom", None),
        P(),
        P(),
        P(),
        P("dom", "ens", None, None),
        P("dom", "ens", None, None),
    )
    return jax.shard_map(
        local, mesh=mesh, in_specs=placed, out_specs=P("dom", "ens", None, None), check_vma=False
    )
```

```python
import jax
import jax.numpy as jnp
from jax import lax
from jax.experimental import pallas as pl
from jax.experimental.pallas import tpu as pltpu
from jax.sharding import PartitionSpec as P

F32 = jnp.float32
BF16 = jnp.bfloat16
EXTRA = 256
PACKED_ROWS = EXTRA + 8
NT = (((1,), (1,)), ((), ()))
NN = (((1,), (0,)), ((), ()))


def split2(value):
    high = value.astype(BF16)
    low = (value - high.astype(F32)).astype(BF16)
    return high, low


def dot3(left, right, dims=NN):
    def one(a, b):
        return lax.dot_general(a, b, dims, preferred_element_type=F32)

    return one(left[0], right[0]) + (one(left[0], right[1]) + one(left[1], right[0]))


def dot3_rows(left, right):
    rows = left[0].shape[0]
    both = jnp.dot(jnp.concatenate(left, axis=0), right[0], preferred_element_type=F32)
    return both[:rows] + (both[rows:] + jnp.dot(left[0], right[1], preferred_element_type=F32))


def iota2(shape, axis):
    return lax.broadcasted_iota(jnp.int32, shape, axis)


def block_kernel(*refs):
    parts = refs[:8]
    scaled_ref, out_ref, high_ref, low_ref, heavy_high_ref, heavy_low_ref = refs[8:]
    place = lax.axis_index("ens")
    chip, core = place // 2, lax.rem(place, 2)
    inverse = scaled_ref[0:1, :]
    for index, part in enumerate(parts):
        side = core if index < 4 else 1 - core
        behind = lax.rem(chip + (0, 3, 1, 2)[index % 4], 4)
        at = pl.ds(pl.multiple_of(side * 128 + behind * 32, 32), 32)
        value = part[...]
        high_ref[at, :], low_ref[at, :] = split2(value)
        heavy_high_ref[at, :], heavy_low_ref[at, :] = split2(value * inverse)
    pull = split2(jnp.broadcast_to(scaled_ref[1:2, :], (16, scaled_ref.shape[1])))
    heavy = (
        jnp.concatenate([heavy_high_ref[...], pull[0]], axis=0),
        jnp.concatenate([heavy_low_ref[...], pull[1]], axis=0),
    )
    product = dot3(heavy, (high_ref[...], low_ref[...]), NT)
    row, col = iota2((64, 128), 0), iota2((64, 128), 1)
    extra_row = iota2((8, 128), 0)
    extra = jnp.zeros((8, 128), F32)
    for side in range(2):
        lanes = slice(side * 128, side * 128 + 128)
        top = product[side * 128 : side * 128 + 64, lanes]
        bottom = pltpu.roll(product[side * 128 + 64 : side * 128 + 128, lanes], 64, 1)
        base = side * 128
        out_ref[base : base + 64, :] = jnp.where((col < 64) & (col > row), bottom, top)
        out_ref[base + 64 : base + 128, :] = product[side * 64 : side * 64 + 64, 128:]
        diagonal = jnp.sum(jnp.where(row == col, bottom, 0.0), axis=0, keepdims=True)
        extra = jnp.where(extra_row == 2 * side, diagonal, extra)
        extra = jnp.where(extra_row == 2 * side + 1, product[256:257, lanes], extra)
    out_ref[EXTRA:PACKED_ROWS, :] = extra


def add_tiles(weight_ref, tiles, start_ref, out_ref):
    for band in range(5):
        at = pl.ds(band * 56, 56 if band < 4 else 40)
        for pair in range(2):
            totals = [None if start_ref is None else start_ref[2 * pair + side, at, :] for side in range(2)]
            for ref, offset, block in tiles:
                tile = ref[at, :]
                for side in range(2):
                    row = (2 * pair + side) * 20 + offset * 4 + block
                    term = tile * weight_ref[pl.ds(row, 1), :]
                    totals[side] = term if totals[side] is None else totals[side] + term
            for side in range(2):
                out_ref[2 * pair + side, at, :] = totals[side]


def places():
    place = lax.axis_index("ens")
    chip, core = place // 2, lax.rem(place, 2)
    near = lax.rem(chip + 3 - 2 * core, 4)
    swapped = lax.rem(chip + 1 + 2 * core, 4)
    return core, chip, near, swapped, lax.rem(chip + 2, 4)


def early_kernel(weight_ref, same, far, far_opposite, out_ref):
    core, chip, near, _, ahead = places()
    tiles = [
        (same.at[1], 2, near),
        (same.at[3 * core], 2, lax.rem(chip + 2 * core, 4)),
        (far, 4 * core, chip),
        (far_opposite, 4 * core, ahead),
    ]
    add_tiles(weight_ref, tiles, None, out_ref)


def late_kernel(weight_ref, start_ref, beside, far_near, out_ref):
    core, chip, near, swapped, ahead = places()
    tiles = [
        *[(beside.at[i], 1 + 2 * core, b) for i, b in enumerate((chip, near, swapped, ahead))],
        (far_near.at[0], 4 * core, near),
        (far_near.at[1], 4 - 4 * core, near),
    ]
    add_tiles(weight_ref, tiles, start_ref, out_ref)


def unpack_square(packed, diagonal):
    row, col = iota2((64, 128), 0), iota2((64, 128), 1)
    flipped = jnp.transpose(jnp.concatenate([packed, jnp.zeros_like(packed)], axis=0))
    top = jnp.where((col < 64) & (col > row), flipped[:64], packed)
    upper = pltpu.roll(packed, 64, 1)
    lower = pltpu.roll(flipped[:64], 64, 1)
    middle = pltpu.roll(jnp.broadcast_to(diagonal, (64, 128)), 64, 1)
    shifted = col - 64
    corner = jnp.where(shifted > row, upper, jnp.where(shifted < row, lower, middle))
    bottom = jnp.where(col < 64, flipped[64:], corner)
    return jnp.concatenate([top, bottom], axis=0)


def analysis_kernel(mine_ref, theirs_ref, back_ref, out_ref, held, made, in_sem, out_sem):
    points = back_ref.shape[0]

    def chunks():
        for chip in range(4):
            for side in range(2):
                yield chip * 2 + side, (chip * 2 + side) * 32, side * 128 + chip * 32

    def fetch(point, index, outer, inner):
        return pltpu.make_async_copy(
            back_ref.at[point, pl.ds(outer, 32), :],
            held.at[point, pl.ds(inner, 32), :],
            in_sem.at[point, index],
        )

    def leave(point, index, outer, inner):
        return pltpu.make_async_copy(
            made.at[point, pl.ds(inner, 32), :],
            out_ref.at[point, pl.ds(outer, 32), :],
            out_sem.at[point, index],
        )

    for point in range(points):
        for chunk in chunks():
            fetch(point, *chunk).start()

    identity = (iota2((256, 256), 0) == iota2((256, 256), 1)).astype(F32)
    every = range(points)
    start, scale, drives, squares = [], [], [], []
    for point in every:
        whole = mine_ref[point] + theirs_ref[point]
        extra = whole[EXTRA:]
        cross = jnp.concatenate([whole[64:128], whole[192:256]], axis=0)
        corners = [unpack_square(whole[:64], extra[0:1]), unpack_square(whole[128:192], extra[2:3])]
        gram = jnp.concatenate(
            [
                jnp.concatenate([corners[0], cross], axis=1),
                jnp.concatenate([jnp.transpose(cross), corners[1]], axis=1),
            ],
            axis=0,
        )
        system = 255.0 * identity + gram
        inverse_norm = lax.rsqrt(jnp.sum(system * system, axis=(0, 1), keepdims=True))
        system_pair = split2(system)
        squares.append(dot3_rows(system_pair, system_pair) * (inverse_norm * inverse_norm))
        start.append(system * inverse_norm)
        scale.append(inverse_norm)
        drives.append(jnp.concatenate([extra[1:2], extra[3:4]], axis=1))

    def two_steps(value, squared):
        squared_pair = [split2(squared[i]) for i in every]
        rest = [
            split2(1.6875 * identity - 0.5625 * value[i] + 0.0625 * squared[i]) for i in every
        ]
        return [
            dot3_rows(squared_pair[i], rest[i]) + (2.25 * identity - 2.4375 * value[i]) for i in every
        ]

    pair = [split2(start[i]) for i in every]
    root = two_steps(start, squares)
    root_pair = [split2(root[i]) for i in every]
    value = [dot3_rows(split2(dot3_rows(pair[i], root_pair[i])), root_pair[i]) for i in every]
    pair = [split2(value[i]) for i in every]
    factor_pair = [split2(f) for f in two_steps(value, [dot3_rows(pair[i], pair[i]) for i in every])]
    root_pair = [split2(dot3_rows(factor_pair[i], root_pair[i])) for i in every]
    value = [dot3_rows(split2(dot3_rows(pair[i], factor_pair[i])), factor_pair[i]) for i in every]
    pair = [split2(value[i]) for i in every]
    for point in every:
        for chunk in chunks():
            fetch(point, *chunk).wait()
    factor_pair = [split2(f) for f in two_steps(value, [dot3_rows(pair[i], pair[i]) for i in every])]
    root = [dot3_rows(factor_pair[i], root_pair[i]) for i in every]
    for point in every:
        inner = jnp.sum(root[point] * drives[point], axis=1, keepdims=True)
        mean = jnp.sum(root[point] * inner, axis=0, keepdims=True) * scale[point]
        transform = split2(jnp.sqrt(255.0 * scale[point]) * root[point] + mean)
        for part in range(2):
            lanes = pl.ds(part * 512, 512)
            made[point, :, lanes] = dot3_rows(transform, split2(held[point, :, lanes]))
        for chunk in chunks():
            leave(point, *chunk).start()
    for point in every:
        for chunk in chunks():
            leave(point, *chunk).wait()


def along_x(value, steps, swap=0):
    pairs = [(e, ((e // 2 + steps) % 4) * 2 + ((e % 2) ^ swap)) for e in range(8)]
    return lax.ppermute(value, "ens", pairs)


def other_core(value):
    return along_x(value, 0, 1)


def both_ways(value, axis, steps):
    pairs = []
    for e in range(8):
        for t in range(16):
            way = steps if e % 2 == 0 else -steps
            if axis == "dom":
                pairs.append((e * 16 + t, e * 16 + (t + way) % 16))
            else:
                pairs.append((e * 16 + t, (((e // 2 + way) % 4) * 2 + e % 2) * 16 + t))
    return lax.ppermute(value, ("ens", "dom"), pairs)


def block_weights(loc_table, counts, own_picks, loc_index, tile):
    own_counts = lax.dynamic_index_in_dim(counts, tile, 0, keepdims=False)
    bins = jnp.arange(loc_table.shape[0], dtype=jnp.int32)
    four = jnp.arange(4, dtype=jnp.int32)
    live = four[None, :] < own_counts[:, None]
    chosen = live[:, None, :] & (own_picks[:, None, :] == four[None, :, None])
    hit = (loc_index[:, :, None, :, None] == bins) & chosen[None, ..., None]
    weight = jnp.sum(jnp.where(hit, loc_table, 0.0), axis=(3, 4))
    return weight.reshape(loc_index.shape[0], 20)


def local(
    obs_members, innovations, error_inverse, loc_table, counts, block_picks, loc_index, background
):
    place = lax.axis_index("ens")
    tile = lax.axis_index("dom")
    chip = place // 2
    vmem = pl.BlockSpec(memory_space=pltpu.VMEM)

    def block_of(blocks, steps):
        return lax.dynamic_index_in_dim(blocks, lax.rem(chip + steps, 4), 0, keepdims=False)

    inverse = lax.dynamic_slice_in_dim(error_inverse, chip, 1, 0)
    pull = inverse * lax.dynamic_slice_in_dim(innovations, chip, 1, 0)
    scaled = jnp.concatenate([inverse, pull], axis=0)
    order = (1, 3, 2)
    own, *sent = [block_of(obs_members, steps) for steps in (0, *order)]
    own, *sent, loc_index, counts, block_picks = lax.optimization_barrier(
        (own, *sent, loc_index, counts, block_picks)
    )
    parts = [own] + [along_x(part, steps) for part, steps in zip(sent, order)]
    parts = parts + [other_core(part) for part in parts]
    own_picks = lax.dynamic_index_in_dim(block_picks, tile, 0, keepdims=False)
    weight = block_weights(loc_table, counts, own_picks, loc_index[0], tile)
    scaled, weight = lax.optimization_barrier((scaled, weight))
    whole = pl.pallas_call(
        block_kernel,
        out_shape=jax.ShapeDtypeStruct((PACKED_ROWS, 128), F32),
        in_specs=[vmem] * 9,
        out_specs=vmem,
        scratch_shapes=[pltpu.VMEM((256, 1024), BF16)] * 4,
        compiler_params=pltpu.CompilerParams(vmem_limit_bytes=16 << 20),
        name="block_matrices",
    )(*parts, scaled)
    far = both_ways(whole, "dom", 2)
    near = both_ways(whole, "ens", 1)
    opposite = along_x(whole, 2)
    weight = jnp.broadcast_to(weight.reshape(-1, 1), (weight.size, 128))
    weights = [weight, other_core(weight)]
    near, far, opposite, weights = lax.optimization_barrier((near, far, opposite, weights))
    near_swapped, far_swapped = other_core(near), other_core(far)
    same = jnp.stack([whole, near, near_swapped, opposite])
    far_both = jnp.stack([far, far_swapped])
    same, far, far_both = lax.optimization_barrier((same, far, far_both))
    far_opposite = along_x(far, 2)
    far_near = both_ways(far_both, "ens", 1)
    beside = both_ways(same, "dom", 1)
    far_near, beside, far_opposite = lax.optimization_barrier((far_near, beside, far_opposite))
    def combine(kernel, flops, *operands):
        return pl.pallas_call(
            kernel,
            out_shape=jax.ShapeDtypeStruct((4, PACKED_ROWS, 128), F32),
            in_specs=[vmem] * len(operands),
            out_specs=vmem,
            compiler_params=pltpu.CompilerParams(vmem_limit_bytes=16 << 20),
            cost_estimate=pl.CostEstimate(flops=flops, bytes_accessed=2000000, transcendentals=0),
            name=kernel.__name__,
        )(*operands)

    started = [combine(early_kernel, 2000000, part, same, far, far_opposite) for part in weights]
    theirs = other_core(combine(late_kernel, 2000000, weights[1], started[1], beside, far_near))
    mine = combine(late_kernel, 2000000, weights[0], started[0], beside, far_near)
    points, members, cells = background.shape[1:]
    analysis = pl.pallas_call(
        analysis_kernel,
        out_shape=jax.ShapeDtypeStruct((points, members, cells), F32),
        in_specs=[vmem, vmem, pl.BlockSpec(memory_space=pltpu.HBM)],
        out_specs=pl.BlockSpec(memory_space=pltpu.HBM),
        scratch_shapes=[
            pltpu.VMEM((points, members, cells), F32),
            pltpu.VMEM((points, members, cells), F32),
            pltpu.SemaphoreType.DMA((points, 8)),
            pltpu.SemaphoreType.DMA((points, 8)),
        ],
        compiler_params=pltpu.CompilerParams(vmem_limit_bytes=52 << 20),
        name="root_and_analysis",
    )(mine, theirs, background[0])
    return analysis[None]


def solution(mesh):
    placed = (
        P("dom", "ens", None),
        P("dom", None),
        P("dom", None),
        P(),
        P(),
        P(),
        P("dom", "ens", None, None),
        P("dom", "ens", None, None),
    )
    return jax.shard_map(
        local, mesh=mesh, in_specs=placed, out_specs=P("dom", "ens", None, None), check_vma=False
    )
```
